128 devices in a mesh: sub: 4 (over x), row: 4 (over z), col: 8 (over y, core).
Axes of the slice: x: 4, y: 4, z: 4, core: 2. Of those that a mesh axis runs over, the one named last changes fastest.
Arguments:
- parent_front: float32 [16384, 16384], P(('sub', 'row'), 'col')
- child_panel: float32 [4, 8192, 512], P('sub', 'row'), may hold values from -0.25 to 0.25
- child_pattern: int32 [4, 64, 4], P('sub', 'row'), may hold values 0 or 1
- child_map: int32 [4, 64], replicated, may hold values from 0 to 127, as said below
Outputs:
- schur_block: float32 [16384, 16384], P(('sub', 'row'), 'col')
- panel_factor: float32 [16384, 512], P(('sub', 'row'))
The draws below stay inside these ranges and needn't reach their ends.
Inputs may be any that keep to these rules, and one draw needn't show every extreme that they name: `child_map`: within a child the values are distinct. Child block i, with r = i // (2 * 8), c = (i // 2) % 8 and e = i % 2, maps into parent blocks c * 16 to (c + 1) * 16 - 1, and within one child and one c the value rises with e * 4 + r. Hence at most 2 of the blocks i with one r and one c fall in one row group of 8 parent blocks; in every draw some row group receives exactly 2 such blocks from every r and every child.
All inputs are finite; a program needn't handle non-finite values. No bound on the sum of `child_pattern` on one device may be relied on, other than what follows from the above.
Results may differ from the reference program's by a relative error of at most 0.0001.
Values sent between devices are 32-bit elements; how exact they have to be, the bound alone decides.
No kernel may reach another device: no remote copies, remote signals or barrier semaphores. Data moves between devices by JAX's collectives and lax.ppermute only.
A program may use at most 128 MiB of HBM per device.

```python
import jax
import jax.numpy as jnp
from jax import lax

B = 128
K = 512
E = 2
PW = 4
NG = 16
GPC = 2
RB = 8
PCB = 16
CB = 64
NP = 16384
NC = 8192
KB = 4
N_SUB = 4
N_ROW = 4
N_COL = 8


def draw_parent_front(key, part):
    entry_key, diag_key = jax.random.split(key)
    entries = jax.random.uniform(entry_key, (NP, NP), jnp.float32, -0.2, 0.2)
    diagonal = 32.0 + 32.0 * jax.random.uniform(diag_key, (NP,), jnp.float32)
    symmetric = 0.5 * (entries + entries.T)
    places = jnp.arange(NP, dtype=jnp.int32)
    return symmetric.at[places, places].add(diagonal)


def draw_child_map(key, part):
    dense_key, pick_key = jax.random.split(key)
    dense_group = jax.random.randint(dense_key, (), 0, NG)
    dense_group = jnp.where(dense_group // GPC == N_COL - 1, NG - 1, dense_group)
    dense_col = dense_group // GPC
    dense_start = dense_group % GPC * RB
    pair_keys = jax.random.split(pick_key, N_SUB * N_COL)

    def choose_blocks(one_key):
        shuffled = jax.random.permutation(one_key, PCB - 1)
        picks = jnp.concatenate([shuffled[:RB - 1], jnp.full((1,), PCB - 1, shuffled.dtype)])
        return jnp.sort(picks)
    chosen = jax.vmap(choose_blocks)(pair_keys).reshape(N_SUB, N_COL, RB)
    col_range = jnp.arange(N_COL, dtype=jnp.int32)
    dense_rows = dense_start + jnp.arange(RB, dtype=jnp.int32)
    chosen = jnp.where((col_range == dense_col)[None, :, None], dense_rows[None, None, :], chosen)
    parent = chosen + (col_range * PCB)[None, :, None]
    parent = parent.reshape(N_SUB, N_COL, E, N_ROW)
    return parent.transpose(0, 3, 1, 2).reshape(N_SUB, CB).astype(jnp.int32)


def with_ends(values, rng, least, largest):
    shape = values.shape
    place = [jax.random.randint(jax.random.fold_in(rng, axis), (), 0, shape[axis]) for axis in range(len(shape))]
    values = values.at[tuple(place)].set(least)
    longest = shape.index(max(shape))
    place[longest] = (place[longest] + 1) % shape[longest]
    return values.at[tuple(place)].set(largest)


def level_of(stream_key, dims, shards, least, top_value):
    def one(dim, blocks):
        steps = jax.random.uniform(jax.random.fold_in(jax.random.fold_in(stream_key, 6), dim), (blocks,), jnp.float32, least / len(shards), top_value / len(shards))
        return jnp.repeat(jnp.exp(steps), dims[dim] // blocks).reshape((-1,) + (1,) * (len(dims) - dim - 1))

    loudness = one(*shards[0])
    for cut in shards[1:]:
        loudness = loudness * one(*cut)
    return loudness


def bell_draw(stream_key, shape, deviation, most, pieces=(), held_as=jnp.bfloat16):
    values = jax.random.normal(stream_key, shape, jnp.float32) * deviation
    if len(pieces) > 0:
        values = level_of(stream_key, shape, pieces, -0.22, 0.18) * values
    return jnp.clip(values, min=-most, max=most).astype(held_as)


def setup_inputs(seed: int = 0) -> dict:
    streams_of = jax.random.split(jax.random.key(seed), 5)
    return {
        "parent_front": draw_parent_front(jax.random.fold_in(streams_of[4], 71), 0),
        "child_panel": bell_draw(streams_of[1], (N_SUB, NC, K), K ** -0.5, 0.25, ((0, 4), (1, 4)), jnp.float32),
        "child_pattern": with_ends((jax.random.randint(streams_of[2], (N_SUB, CB, KB), 0, 4) < 3).astype(jnp.int32), jax.random.fold_in(streams_of[2], 1), 0, 1),
        "child_map": draw_child_map(jax.random.fold_in(streams_of[4], 71), 0),
    }


def reference(parent_front, child_panel, child_pattern, child_map):
    blocks_k = K // B
    offsets = jnp.arange(B, dtype=jnp.int32)
    assembled = parent_front
    for child in range(N_SUB):
        pattern = child_pattern[child].astype(jnp.float32)
        masked = (child_panel[child].reshape(CB, B, blocks_k, B) * pattern[:, None, :, None]).reshape(CB * B, K)
        update = jnp.dot(masked.astype(jnp.float32), masked.T.astype(jnp.float32), precision=lax.Precision.HIGHEST, preferred_element_type=jnp.float32)
        indices = (child_map[child][:, None] * B + offsets[None, :]).reshape(-1).astype(jnp.int32)
        assembled = assembled.at[indices[:, None], indices[None, :]].add(-update)
    panel_width = PW * B
    factor_top = jnp.linalg.cholesky(assembled[:panel_width, :panel_width])
    solved = jax.scipy.linalg.solve_triangular(factor_top, assembled[:, :panel_width].T, lower=True).T
    factor = solved.at[:panel_width].set(factor_top)
    schur_block = assembled - jnp.dot(factor.astype(jnp.float32), factor.T.astype(jnp.float32), precision=lax.Precision.HIGHEST, preferred_element_type=jnp.float32)
    return (schur_block, factor)
```

```python
import jax
import jax.numpy as jnp
from jax import lax
from jax.experimental import pallas as pl
from jax.experimental.pallas import tpu as pltpu
from jax.sharding import PartitionSpec as P

B = 128
K = 512
E = 2
PW = 512
ALL = ("sub", "row", "col")
NS, NR, NC = 4, 4, 8
OFFS = (0, 3, 1, 2)
F32 = jnp.float32
BF16 = jnp.bfloat16
MIB = 1 << 20


def gid(s, r, c):
    return (s * NR + r) * NC + c


DEVICES = [(s, r, c) for s in range(NS) for r in range(NR) for c in range(NC)]


def moved(axis, k, s, r, c):
    if axis == "x":
        return ((s + k) % NS, r, c)
    if axis == "z":
        return (s, (r + k) % NR, c)
    if axis == "y":
        return (s, r, (c + 2 * k) % NC)
    return (s, r, c ^ 1)


def axis_of(phase, c):
    return "zx"[(phase + c % 2) % 2]


def pairs(phase, k, where=lambda s, r, c: True):
    return [
        (gid(s, r, c), gid(*moved(axis_of(phase, c), k, s, r, c)))
        for s, r, c in DEVICES
        if where(s, r, c)
    ]


def move_pairs(axis, k, where=lambda s, r, c: True):
    return [(gid(s, r, c), gid(*moved(axis, k, s, r, c))) for s, r, c in DEVICES if where(s, r, c)]


def permute(x, prs):
    return lax.ppermute(x, ALL, prs)


def ring_phase(x, phase):
    half = x.shape[0] // 2
    up = permute(x, pairs(phase, 1))
    down = permute(x, pairs(phase, -1))
    far_a = permute(up[:half], pairs(phase, 1))
    far_b = permute(down[half:], pairs(phase, -1))
    return jnp.concatenate([x, up, down, far_a, far_b], axis=0)


def ring_gather(x):
    return ring_phase(ring_phase(x, 0), 1)


def split(x):
    hi = x.astype(BF16)
    lo = (x - hi.astype(F32)).astype(BF16)
    return hi, lo


def left_cat(x):
    hi, lo = split(x)
    return jnp.concatenate([hi, lo, hi], axis=1)


def right_cat(x):
    hi, lo = split(x)
    return jnp.concatenate([hi, hi, lo], axis=1)


def dot_t(a, b, precision=None):
    return lax.dot_general(
        a, b, (((1,), (1,)), ((), ())), precision=precision, preferred_element_type=F32
    )


def offset(p):
    return jnp.where(p == 0, 0, jnp.where(p == 1, 3, jnp.where(p == 2, 1, 2)))


def factor_block(rows):
    n = len(rows)
    w = list(rows)
    lane = lax.broadcasted_iota(jnp.int32, (8, B), 1)
    sub = lax.broadcasted_iota(jnp.int32, (8, B), 0)
    upper = [None] * n
    for j in range(0, B, 4):
        k0, o = j // 8, j % 8
        cols = [
            [jnp.broadcast_to(w[k][:, j + m : j + m + 1], (8, B)) for m in range(4)]
            for k in range(k0, n)
        ]
        top = cols[0]

        def elem(p, q):
            return jnp.broadcast_to(top[q][o + p : o + p + 1, :], (8, B))

        l = {}
        inv = [None] * 4
        for q in range(4):
            d = elem(q, q)
            for t in range(q):
                d = d - l[q, t] * l[q, t]
            y = lax.rsqrt(d)
            inv[q] = y * (1.5 - 0.5 * d * y * y)
            l[q, q] = d * inv[q]
            for p in range(q + 1, 4):
                e = elem(p, q)
                for t in range(q):
                    e = e - l[p, t] * l[q, t]
                l[p, q] = e * inv[q]
        in_block = (lane >= j) & (lane < j + 4)
        orig = [jnp.broadcast_to(w[k0][o + m : o + m + 1, :], (8, B)) for m in range(4)]
        ident = [
            jnp.where(in_block, jnp.where(lane == j + m, 1.0, 0.0).astype(F32), orig[m])
            for m in range(4)
        ]
        uo, ui = [], []
        for m in range(4):
            a, b = orig[m], ident[m]
            for t in range(m):
                a = a - l[m, t] * uo[t]
                b = b - l[m, t] * ui[t]
            uo.append(a * inv[m])
            ui.append(b * inv[m])
        back = [None] * 4
        for m in (3, 2, 1, 0):
            a = ui[m]
            for t in range(m + 1, 4):
                a = a - l[t, m] * back[t]
            back[m] = a * inv[m]
        acc_u = upper[k0] if upper[k0] is not None else jnp.zeros((8, B), F32)
        new_rows = w[k0]
        for m in range(4):
            at = sub == o + m
            acc_u = jnp.where(at & (lane >= j + m), uo[m], acc_u)
            new_rows = jnp.where(at, ui[m], new_rows)
        upper[k0] = acc_u
        for k in range(k0, n):
            if k == k0 and o == 4:
                w[k] = new_rows
                continue
            c = cols[k - k0]
            x = jnp.where(in_block, 0.0, w[k])
            x = x - (c[0] * back[0] + c[1] * back[1]) - (c[2] * back[2] + c[3] * back[3])
            w[k] = jnp.where(sub >= 4, x, new_rows) if k == k0 else x
    for k in range(n):
        w[k] = jnp.where(lane <= sub + 8 * k, w[k], 0.0)
    return upper, w


def corner_kernel(idx, cmap, corner, q, l_out, li_out, x_out, w, ut, xs):
    s, r, c = idx[0], idx[1], idx[2]
    core = c % 2
    y = c // 2
    for kk in range(2):
        for p in range(4):
            at = 64 * (2 * ((y + OFFS[p]) % 4) + (core if kk == 0 else 1 - core))
            w[pl.ds(pl.multiple_of(at, 64), 64), :] = corner[kk * 4 + p]
    xs[...] = jnp.zeros_like(xs)
    for i in range(4):
        child = (s + OFFS[i]) % 4
        for j in range(4):
            row = (r + OFFS[j]) % 4
            slot = cmap[child * 64 + row * 16]
            chunk = jnp.where(core == 0, i * 4 + j, j * 4 + i)

            @pl.when(slot < 4)
            def _():
                hi, lo = split(q[chunk])
                at = pl.ds(pl.multiple_of(slot * B, B), B)
                xs[i, at, 0:K] = hi
                xs[i, at, K : 2 * K] = lo
    for i in range(4):
        hi, lo = xs[i, :, 0:K], xs[i, :, K : 2 * K]
        x_out[i, :, 0:K] = hi
        x_out[i, :, K : 2 * K] = hi
        x_out[i, :, 2 * K :] = lo
        a = jnp.concatenate([hi, lo, hi], axis=1)
        b = jnp.concatenate([hi, hi, lo], axis=1)
        w[...] -= dot_t(a, b)

    col = lax.broadcasted_iota(jnp.int32, (B, PW), 1)
    row = lax.broadcasted_iota(jnp.int32, (B, B), 0)
    col_b = lax.broadcasted_iota(jnp.int32, (B, B), 1)
    eye = jnp.where(row == col_b, 1.0, 0.0).astype(F32)

    def stage(b, carry):
        o = pl.multiple_of(b * B, B)
        blk = pl.ds(o, B)
        diag = w[blk, blk]
        upper, inv = factor_block([diag[8 * k : 8 * k + 8, :] for k in range(16)])
        inv = jnp.concatenate(inv, axis=0)
        w[blk, blk] = eye
        u = jnp.dot(inv, w[blk, :], precision=lax.Precision.HIGHEST, preferred_element_type=F32)
        right = jnp.where(col >= o + B, u, 0.0)
        ut[blk, :] = right
        ut[blk, blk] = jnp.concatenate(upper, axis=0)
        w[:, blk] = jnp.zeros((PW, B), F32)
        w[...] -= lax.dot_general(
            right,
            u,
            (((0,), (0,)), ((), ())),
            precision=lax.Precision.HIGHEST,
            preferred_element_type=F32,
        )
        w[blk, :] = u
        return carry

    lax.fori_loop(0, 4, stage, 0)
    rows = lax.broadcasted_iota(jnp.int32, (PW, PW), 0)
    cols = lax.broadcasted_iota(jnp.int32, (PW, PW), 1)
    li_out[...] = right_cat(jnp.where(cols <= rows, w[...], 0.0))
    l_out[...] = ut[...].T


def tile_kernel(
    idx, cmap, s0, s1, s2, s3, rows_ref, pg_ref, x_ref, l_ref, li_ref, parent, out, own_out,
    acc, pg, pc, rcat, ocat, fcat, sem,
):
    s, r, c = idx[0], idx[1], idx[2]
    core = c % 2
    group = s * 4 + r
    i = pl.program_id(0)
    tile_rows, tile_cols = parent.shape
    load = pltpu.make_async_copy(parent, acc.at[pl.ds(0, tile_rows), :], sem.at[0])

    @pl.when(i == 0)
    def _():
        load.start()
        pc[...] = jnp.zeros_like(pc)
        for o in range(8):
            pg[pl.ds(64 * o, 64), :] = pg_ref[o, 0:64, :]
            pg[pl.ds(512 + 64 * o, 64), :] = pg_ref[o, 64:128, :]

    child = (s + offset(i)) % 4
    rcat[...] = left_cat(rows_ref[...].reshape(tile_rows, K))
    x = x_ref[0]

    def row_slot(rr, e):
        v = cmap[child * 64 + rr * 16 + (group // 2) * 2 + e] - group * 8
        return jnp.where((v >= 0) & (v < 8), v, 8)

    def to_rows(dst, value, cols):
        for rr in range(4):
            for e in range(2):
                at = row_slot(rr, e) * B
                for part in range(4):
                    src = (4 * e + part) * B + rr * 32
                    d = pl.ds(pl.multiple_of(at + 32 * part, 32), 32)
                    dst[d, cols] -= value[src : src + 32, :]

    for h in range(2):
        cols = slice(256 * h, 256 * h + 256)
        to_rows(pg, dot_t(rcat[...], x_ref[0, cols, :]), cols)

    @pl.when(i == 0)
    def _():
        load.wait()

    for j, piece in enumerate((s0, s1, s2, s3)):
        rr = (r + OFFS[j]) % 4
        p_sub = jnp.where(core == 0, child, child)
        shard = (p_sub * 4 + rr)
        at = (shard // 8) * 1024 + 64 * (shard % 8)
        pc[pl.ds(pl.multiple_of(at, 64), 64), :] += piece[0, 256:320, :]
        pc[pl.ds(pl.multiple_of(at + 512, 64), 64), :] += piece[0, 320:384, :]
        hi, lo = split(piece[0, 0:256, :])
        scat = jnp.concatenate([hi, hi, lo], axis=1)
        prod = dot_t(rcat[...], scat)
        up = dot_t(jnp.concatenate([hi, lo, hi], axis=1), x)
        for e in range(2):
            slot = cmap[child * 64 + rr * 16 + c * 2 + e] - c * 16
            at = pl.multiple_of(slot * B, B)
            pc[pl.ds(at, B), :] -= up[B * e : B * e + B, :]
            to_rows(acc, prod[:, B * e : B * e + B], pl.ds(at, B))

    @pl.when(i == 3)
    def _():
        li = li_ref[...]
        own = dot_t(left_cat(pg[pl.ds(0, tile_rows), :]), li)
        pg[pl.ds(0, tile_rows), :] = own

        @pl.when(group == 0)
        def _():
            pg[pl.ds(0, PW), :] = l_ref[...]

        ocat[...] = left_cat(pg[pl.ds(0, tile_rows), :])
        send_own = pltpu.make_async_copy(pg.at[pl.ds(0, tile_rows), :], own_out, sem.at[1])
        send_own.start()
        for n in range(tile_cols // 256):
            cols = pl.ds(256 * n, 256)
            far = dot_t(left_cat(pc[cols, :]), li)
            if n < 2:
                far = jnp.where(c == 0, l_ref[cols, :], far)
            fcat[...] = right_cat(far)
            acc[pl.ds(0, tile_rows), cols] -= dot_t(ocat[...], fcat[...])
            pltpu.make_async_copy(
                acc.at[pl.ds(0, tile_rows), cols], out.at[:, cols], sem.at[2]
            ).start()
        pltpu.make_async_copy(acc.at[pl.ds(0, tile_rows), :], out, sem.at[2]).wait()
        send_own.wait()


def per_device(parent_front, child_panel, child_pattern, child_map):
    s = lax.axis_index("sub")
    r = lax.axis_index("row")
    c = lax.axis_index("col")
    y, core = c // 2, c % 2
    idx = jnp.stack([s, r, c]).astype(jnp.int32)
    cmap = child_map.reshape(-1)
    tile_rows, tile_cols = parent_front.shape
    panel = child_panel[0]
    weights = jnp.repeat(child_pattern[0].astype(F32), B, axis=1)

    q = ring_gather(panel[:B] * weights[0][None, :])

    slabs = parent_front[:, :PW].reshape(2, 8, 64, PW).transpose(1, 0, 2, 3).reshape(4, 2, B, PW)
    mate = permute(slabs[:, 1], move_pairs("k", 1, lambda s, r, c: c == 0))
    mine = jnp.where(core == 0, slabs[:, 0], mate)
    near_y = lambda s, r, c: c < 2
    share = jnp.where(y == 0, mine[0], jnp.zeros_like(mine[0]))
    for k in (1, 3, 2):
        share = share + permute(mine[k], move_pairs("y", k, near_y))

    slab = share[:64]
    at_root = (lambda s, r, c: s == 0 and r == 0)
    on_line = (lambda s, r, c: (s == 0) if c % 2 else (r == 0))

    def first_axis_is_root(s, r, c):
        return s == 0 and r == 0

    def second_axis_is_root(s, r, c):
        return r == 0 if axis_of(1, c) == "z" else s == 0

    here = jnp.where((s == 0) & (r == 0), slab, jnp.zeros_like(slab))
    one = here
    for k in (1, 3, 2):
        one = one + permute(here, pairs(0, k, first_axis_is_root))
    two = one
    for k in (1, 3, 2):
        two = two + permute(one, pairs(1, k, second_axis_is_root))
    ring_y = [two] + [permute(two, move_pairs("y", k)) for k in (1, 3, 2)]
    ring_y = jnp.stack([ring_y[0], ring_y[1], ring_y[2], ring_y[3]])
    corner = jnp.concatenate([ring_y, permute(ring_y, move_pairs("k", 1))], axis=0)

    oct_rows = lax.dynamic_slice_in_dim(panel.reshape(8, 8, 32, K), c, 1, 1)[:, 0]
    oct_w = weights.reshape(8, 2, K)
    oct_w = jnp.where(c >= 4, oct_w[:, 1], oct_w[:, 0])
    outgoing = jnp.repeat(oct_rows * oct_w[:, None, :], 2, axis=0)
    arrived = lax.all_to_all(outgoing, ("sub", "row"), split_axis=0, concat_axis=0, tiled=True)
    row_share = jnp.concatenate([arrived.reshape(16 * 32, K), share], axis=0)
    row_data = lax.all_gather(row_share, "col", axis=0, tiled=False)

    to_shard = []
    for g in range(16):
        for cc in range(8):
            b = 8 * g + cc
            to_shard.append((g * 8 + cc, (b % 16) * 8 + b // 16))
    panel_share = permute(share, to_shard)
    own_rows = lax.dynamic_slice_in_dim(panel, c * (E * B), E * B, 0).reshape(E, B, K)
    own_w = lax.dynamic_slice_in_dim(weights, c * E, E, 0)
    col_share = jnp.concatenate([(own_rows * own_w[:, None, :]).reshape(E * B, K), panel_share], axis=0)
    col_data = ring_gather(col_share).reshape(16, 3 * B, K)

    vmem = pl.BlockSpec(memory_space=pltpu.VMEM)
    smem = pl.BlockSpec(memory_space=pltpu.SMEM)
    lower, lower_inv, x_cat = pl.pallas_call(
        corner_kernel,
        in_specs=[smem, smem, vmem, vmem],
        out_specs=[vmem, vmem, vmem],
        out_shape=[
            jax.ShapeDtypeStruct((PW, PW), F32),
            jax.ShapeDtypeStruct((PW, 3 * PW), BF16),
            jax.ShapeDtypeStruct((4, PW, 3 * K), BF16),
        ],
        scratch_shapes=[
            pltpu.VMEM((PW, PW), F32),
            pltpu.VMEM((PW, PW), F32),
            pltpu.VMEM((4, PW, 2 * K), BF16),
        ],
        compiler_params=pltpu.CompilerParams(vmem_limit_bytes=40 * MIB),
        cost_estimate=pl.CostEstimate(flops=60_000_000_000, bytes_accessed=12 * MIB, transcendentals=0),
    )(idx, cmap, corner, q.reshape(16, B, K))

    def chunk_map(j):
        def at(i, idx, cmap):
            first = i * 4 + j
            second = j * 4 + i
            return (jnp.where(idx[2] % 2 == 0, first, second), 0, 0)
        return at

    def child_rows(i, idx, cmap):
        return (0, (idx[0] + offset(i)) % 4, 0)

    hbm = pl.BlockSpec(memory_space=pl.ANY)
    once = pl.Buffered(1)
    schur, own = pl.pallas_call(
        tile_kernel,
        grid_spec=pltpu.PrefetchScalarGridSpec(
            num_scalar_prefetch=2,
            grid=(4,),
            in_specs=[pl.BlockSpec((1, 3 * B, K), chunk_map(j)) for j in range(4)]
            + [
                pl.BlockSpec((8, B, K), child_rows),
                pl.BlockSpec((8, B, K), lambda i, idx, cmap: (0, 4, 0), pipeline_mode=once),
                pl.BlockSpec((1, PW, 3 * K), lambda i, idx, cmap: (i, 0, 0)),
                pl.BlockSpec((PW, PW), lambda i, idx, cmap: (0, 0), pipeline_mode=once),
                pl.BlockSpec((PW, 3 * PW), lambda i, idx, cmap: (0, 0), pipeline_mode=once),
                hbm,
            ],
            out_specs=[hbm, hbm],
            scratch_shapes=[
                pltpu.VMEM((tile_rows + B, tile_cols), F32),
                pltpu.VMEM((tile_rows + B, PW), F32),
                pltpu.VMEM((tile_cols, PW), F32),
                pltpu.VMEM((tile_rows, 3 * K), BF16),
                pltpu.VMEM((tile_rows, 3 * K), BF16),
                pltpu.VMEM((256, 3 * K), BF16),
                pltpu.SemaphoreType.DMA((3,)),
            ],
        ),
        out_shape=[
            jax.ShapeDtypeStruct((tile_rows, tile_cols), F32),
            jax.ShapeDtypeStruct((tile_rows, PW), F32),
        ],
        compiler_params=pltpu.CompilerParams(
            vmem_limit_bytes=56 * MIB, dimension_semantics=("arbitrary",)
        ),
        cost_estimate=pl.CostEstimate(flops=45_000_000_000, bytes_accessed=50 * MIB, transcendentals=0),
    )(idx, cmap, col_data, col_data, col_data, col_data, row_data, row_data, x_cat, lower, lower_inv, parent_front)
    return schur, own


def solution(mesh):
    placed = (P(("sub", "row"), "col"), P("sub", "row", None), P("sub", "row", None), P())
    return jax.shard_map(
        per_device,
        mesh=mesh,
        in_specs=placed,
        out_specs=(P(("sub", "row"), "col"), P(("sub", "row"), None)),
        check_vma=False,
    )
```

```python
import jax
import jax.numpy as jnp
from jax import lax
from jax.experimental import pallas as pl
from jax.experimental.pallas import tpu as pltpu
from jax.sharding import PartitionSpec as P

B = 128
K = 512
E = 2
PW = 512
ALL = ("sub", "row", "col")
NS, NR, NC = 4, 4, 8
OFFS = (0, 3, 1, 2)
F32 = jnp.float32
BF16 = jnp.bfloat16
MIB = 1 << 20


def gid(s, r, c):
    return (s * NR + r) * NC + c


DEVICES = [(s, r, c) for s in range(NS) for r in range(NR) for c in range(NC)]


def moved(axis, k, s, r, c):
    if axis == "x":
        return ((s + k) % NS, r, c)
    if axis == "z":
        return (s, (r + k) % NR, c)
    if axis == "y":
        return (s, r, (c + 2 * k) % NC)
    return (s, r, c ^ 1)


def axis_of(phase, c):
    return "zx"[(phase + c % 2) % 2]


def pairs(phase, k, where=lambda s, r, c: True):
    return [
        (gid(s, r, c), gid(*moved(axis_of(phase, c), k, s, r, c)))
        for s, r, c in DEVICES
        if where(s, r, c)
    ]


def move_pairs(axis, k, where=lambda s, r, c: True):
    return [(gid(s, r, c), gid(*moved(axis, k, s, r, c))) for s, r, c in DEVICES if where(s, r, c)]


def permute(x, prs):
    return lax.ppermute(x, ALL, prs)


def ring_near(x, phase):
    return permute(x, pairs(phase, 1)), permute(x, pairs(phase, -1))


def ring_far(up, down, phase):
    half = up.shape[0] // 2
    return permute(up[:half], pairs(phase, 1)), permute(down[half:], pairs(phase, -1))


def split(x):
    hi = x.astype(BF16)
    lo = (x - hi.astype(F32)).astype(BF16)
    return hi, lo


def left_cat(x):
    hi, lo = split(x)
    return jnp.concatenate([hi, lo, hi], axis=1)


def right_cat(x):
    hi, lo = split(x)
    return jnp.concatenate([hi, hi, lo], axis=1)


def dot_t(a, b, precision=None):
    return lax.dot_general(
        a, b, (((1,), (1,)), ((), ())), precision=precision, preferred_element_type=F32
    )


def offset(p):
    return jnp.where(p == 0, 0, jnp.where(p == 1, 3, jnp.where(p == 2, 1, 2)))


def factor_block(rows):
    n = len(rows)
    w = list(rows)
    lane = lax.broadcasted_iota(jnp.int32, (8, B), 1)
    sub = lax.broadcasted_iota(jnp.int32, (8, B), 0)
    upper = [None] * n
    for j in range(0, B, 4):
        k0, o = j // 8, j % 8
        cols = [
            [jnp.broadcast_to(w[k][:, j + m : j + m + 1], (8, B)) for m in range(4)]
            for k in range(k0, n)
        ]
        top = cols[0]

        def elem(p, q):
            return jnp.broadcast_to(top[q][o + p : o + p + 1, :], (8, B))

        l = {}
        inv = [None] * 4
        for q in range(4):
            d = elem(q, q)
            for t in range(q):
                d = d - l[q, t] * l[q, t]
            y = lax.rsqrt(d)
            inv[q] = y * (1.5 - 0.5 * d * y * y)
            l[q, q] = d * inv[q]
            for p in range(q + 1, 4):
                e = elem(p, q)
                for t in range(q):
                    e = e - l[p, t] * l[q, t]
                l[p, q] = e * inv[q]
        in_block = (lane >= j) & (lane < j + 4)
        orig = [jnp.broadcast_to(w[k0][o + m : o + m + 1, :], (8, B)) for m in range(4)]
        ident = [
            jnp.where(in_block, jnp.where(lane == j + m, 1.0, 0.0).astype(F32), orig[m])
            for m in range(4)
        ]
        uo, ui = [], []
        for m in range(4):
            a, b = orig[m], ident[m]
            for t in range(m):
                a = a - l[m, t] * uo[t]
                b = b - l[m, t] * ui[t]
            uo.append(a * inv[m])
            ui.append(b * inv[m])
        back = [None] * 4
        for m in (3, 2, 1, 0):
            a = ui[m]
            for t in range(m + 1, 4):
                a = a - l[t, m] * back[t]
            back[m] = a * inv[m]
        acc_u = upper[k0] if upper[k0] is not None else jnp.zeros((8, B), F32)
        new_rows = w[k0]
        for m in range(4):
            at = sub == o + m
            acc_u = jnp.where(at & (lane >= j + m), uo[m], acc_u)
            new_rows = jnp.where(at, ui[m], new_rows)
        upper[k0] = acc_u
        for k in range(k0, n):
            if k == k0 and o == 4:
                w[k] = new_rows
                continue
            c = cols[k - k0]
            x = jnp.where(in_block, 0.0, w[k])
            x = x - (c[0] * back[0] + c[1] * back[1]) - (c[2] * back[2] + c[3] * back[3])
            w[k] = jnp.where(sub >= 4, x, new_rows) if k == k0 else x
    for k in range(n):
        w[k] = jnp.where(lane <= sub + 8 * k, w[k], 0.0)
    return upper, w


def factor_stage(b, w, ut):
    col = lax.broadcasted_iota(jnp.int32, (B, PW), 1)
    row = lax.broadcasted_iota(jnp.int32, (B, B), 0)
    col_b = lax.broadcasted_iota(jnp.int32, (B, B), 1)
    eye = jnp.where(row == col_b, 1.0, 0.0).astype(F32)
    o = b * B if isinstance(b, int) else pl.multiple_of(b * B, B)
    blk = pl.ds(o, B)
    diag = w[blk, blk]
    upper, inv = factor_block([diag[8 * k : 8 * k + 8, :] for k in range(16)])
    inv = jnp.concatenate(inv, axis=0)
    w[blk, blk] = eye
    u = jnp.dot(inv, w[blk, :], precision=lax.Precision.HIGHEST, preferred_element_type=F32)
    right = jnp.where(col >= o + B, u, 0.0)
    ut[blk, :] = right
    ut[blk, blk] = jnp.concatenate(upper, axis=0)
    w[:, blk] = jnp.zeros((PW, B), F32)
    w[...] -= lax.dot_general(
        right,
        u,
        (((0,), (0,)), ((), ())),
        precision=lax.Precision.HIGHEST,
        preferred_element_type=F32,
    )
    w[blk, :] = u


def corner_kernel(idx, cmap, corner, q_own, q_mate, w, ut, x_out, xs):
    s, r, c = idx[0], idx[1], idx[2]
    core = c % 2
    y = c // 2
    for kk in range(2):
        for p in range(4):
            at = 64 * (2 * ((y + OFFS[p]) % 4) + (core if kk == 0 else 1 - core))
            w[pl.ds(pl.multiple_of(at, 64), 64), :] = corner[kk * 4 + p]
    xs[...] = jnp.zeros_like(xs)
    ut[...] = jnp.zeros_like(ut)
    for i in range(4):
        child = (s + OFFS[i]) % 4
        for row in range(4):
            slot = cmap[child * 64 + row * 16]

            @pl.when(slot < 4)
            def _():
                for half, ref in ((core, q_own), (1 - core, q_mate)):
                    hi, lo = split(ref[child * 4 + row])
                    at = pl.ds(pl.multiple_of(slot * B + half * 64, 64), 64)
                    xs[i, at, 0:K] = hi
                    xs[i, at, K : 2 * K] = lo
    for i in range(4):
        hi, lo = xs[i, :, 0:K], xs[i, :, K : 2 * K]
        x_out[i, :, 0:K] = hi
        x_out[i, :, K : 2 * K] = hi
        x_out[i, :, 2 * K :] = lo
        a = jnp.concatenate([hi, lo, hi], axis=1)
        b = jnp.concatenate([hi, hi, lo], axis=1)
        w[...] -= dot_t(a, b)

    factor_stage(0, w, ut)


def next_kernel(w_in, ut_in, w, ut):
    w[...] = w_in[...]
    ut[...] = ut_in[...]
    factor_stage(1, w, ut)


def stack_kernel(*refs):
    pieces, out, sem = refs[:-2], refs[-2], refs[-1]
    copies = []
    at = 0
    for k, piece in enumerate(pieces):
        rows = piece.shape[0]
        copies.append(pltpu.make_async_copy(piece, out.at[pl.ds(at, rows), :], sem.at[k]))
        copies[-1].start()
        at += rows
    for copy in copies:
        copy.wait()


def stack_rows(pieces):
    hbm = pl.BlockSpec(memory_space=pltpu.HBM)
    rows = sum(x.shape[0] for x in pieces)
    width = pieces[0].shape[1]
    return pl.pallas_call(
        stack_kernel,
        in_specs=[hbm] * len(pieces),
        out_specs=pl.BlockSpec(memory_space=pltpu.VMEM),
        out_shape=jax.ShapeDtypeStruct((rows, width), F32),
        compiler_params=pltpu.CompilerParams(vmem_limit_bytes=16 * MIB),
        scratch_shapes=[pltpu.SemaphoreType.DMA((len(pieces),))],
        cost_estimate=pl.CostEstimate(flops=0, bytes_accessed=8 * rows * width, transcendentals=0),
    )(*pieces)


def finish_kernel(w_in, ut_in, l_out, li_out, w, ut):
    w[...] = w_in[...]
    ut[...] = ut_in[...]

    @pl.loop(2, 4)
    def _(b):
        factor_stage(b, w, ut)

    rows = lax.broadcasted_iota(jnp.int32, (PW, PW), 0)
    cols = lax.broadcasted_iota(jnp.int32, (PW, PW), 1)
    li_out[...] = right_cat(jnp.where(cols <= rows, w[...], 0.0))
    l_out[...] = ut[...].T


def tile_kernel(
    idx, cmap, rows_a, rows_b, pg_a, pg_b, x_ref, l_ref, li_ref, c0, c1, c2, c3a, c3b, parent, out, own_out,
    acc, pg, pc, rcat, ocat, fcat, sbuf, sem, ssem,
):
    s, r, c = idx[0], idx[1], idx[2]
    core = c % 2
    group = s * 4 + r
    i = pl.program_id(0)
    tile_rows, tile_cols = parent.shape
    load = pltpu.make_async_copy(parent, acc.at[pl.ds(0, tile_rows), :], sem.at[0])
    slot = lax.rem(i, 2)
    y = c // 2

    def octant(kk, p):
        return 2 * ((y + OFFS[p]) % 4) + (core if kk == 0 else 1 - core)

    def chunk(piece, n):
        ref = (c0, c1, c2, (c3a, c3b)[n // 2])[piece]
        n = n % 2 if piece == 3 else n
        return ref.at[pl.ds(3 * B * n, 3 * B), :]

    def fetch(step):
        for n in range(4):
            for j in range(4):
                to = sbuf.at[n % 2, j]

                @pl.when((step == n) & (core == 0))
                def _():
                    pltpu.make_async_copy(chunk(n, j), to, ssem.at[n % 2, j]).start()

                @pl.when((step == n) & (core == 1))
                def _():
                    pltpu.make_async_copy(chunk(j, n), to, ssem.at[n % 2, j]).start()

    @pl.when(i == 0)
    def _():
        fetch(i)
        load.start()
        pc[...] = jnp.zeros_like(pc)
        for kk, ref in ((0, pg_a), (1, pg_b)):
            for p in range(4):
                at = 64 * octant(kk, p)
                pg[pl.ds(pl.multiple_of(at, 64), 64), :] = ref[p, 0:64, :]
                pg[pl.ds(pl.multiple_of(at + 512, 64), 64), :] = ref[p, 64:128, :]

    fetch(i + 1)
    child = (s + offset(i)) % 4
    for kk, ref in ((0, rows_a), (1, rows_b)):
        for p in range(4):
            o = octant(kk, p)
            part = left_cat(ref[p])
            for rr in range(4):
                at = pl.multiple_of((2 * rr + o // 4) * B + 32 * (o % 4), 32)
                rcat[pl.ds(at, 32), :] = part[32 * rr : 32 * rr + 32, :]
    x = x_ref[0]

    def row_slot(rr, e):
        v = cmap[child * 64 + rr * 16 + (group // 2) * 2 + e] - group * 8
        return jnp.where((v >= 0) & (v < 8), v, 8)

    places = [pl.multiple_of(row_slot(rr, e) * B, B) for rr in range(4) for e in range(2)]

    def to_rows(dst, value, cols):
        for n, at in enumerate(places):
            dst[pl.ds(at, B), cols] -= value[B * n : B * n + B, :]

    for h in range(2):
        cols = slice(256 * h, 256 * h + 256)
        to_rows(pg, dot_t(rcat[...], x_ref[0, cols, :]), cols)

    @pl.when(i == 0)
    def _():
        load.wait()

    for j in range(4):
        pltpu.make_async_copy(chunk(0, 0), sbuf.at[slot, j], ssem.at[slot, j]).wait()
        piece = sbuf.at[slot, pl.ds(j, 1)]
        rr = (r + OFFS[j]) % 4
        shard = child * 4 + rr
        at = (shard // 8) * 1024 + 64 * (shard % 8)
        pc[pl.ds(pl.multiple_of(at, 64), 64), :] += piece[0, 256:320, :]
        pc[pl.ds(pl.multiple_of(at + 512, 64), 64), :] += piece[0, 320:384, :]
        hi, lo = split(piece[0, 0:256, :])
        scat = jnp.concatenate([hi, hi, lo], axis=1)
        prod = dot_t(rcat[...], scat)
        up = dot_t(jnp.concatenate([hi, lo, hi], axis=1), x)
        for e in range(2):
            place = cmap[child * 64 + rr * 16 + c * 2 + e] - c * 16
            at = pl.multiple_of(place * B, B)
            pc[pl.ds(at, B), :] -= up[B * e : B * e + B, :]
            to_rows(acc, prod[:, B * e : B * e + B], pl.ds(at, B))

    @pl.when(i == 3)
    def _():
        li = li_ref[...]
        own = dot_t(left_cat(pg[pl.ds(0, tile_rows), :]), li)
        pg[pl.ds(0, tile_rows), :] = own

        @pl.when(group == 0)
        def _():
            pg[pl.ds(0, PW), :] = l_ref[...]

        ocat[...] = left_cat(pg[pl.ds(0, tile_rows), :])
        send_own = pltpu.make_async_copy(pg.at[pl.ds(0, tile_rows), :], own_out, sem.at[1])
        send_own.start()
        for n in range(tile_cols // 256):
            cols = pl.ds(256 * n, 256)
            far = dot_t(left_cat(pc[cols, :]), li)
            if n < 2:
                far = jnp.where(c == 0, l_ref[cols, :], far)
            fcat[...] = right_cat(far)
            acc[pl.ds(0, tile_rows), cols] -= dot_t(ocat[...], fcat[...])
            pltpu.make_async_copy(
                acc.at[pl.ds(0, tile_rows), cols], out.at[:, cols], sem.at[2]
            ).start()
        pltpu.make_async_copy(acc.at[pl.ds(0, tile_rows), :], out, sem.at[2]).wait()
        send_own.wait()


def per_device(parent_front, child_panel, child_pattern, child_map):
    s = lax.axis_index("sub")
    r = lax.axis_index("row")
    c = lax.axis_index("col")
    y, core = c // 2, c % 2
    idx = jnp.stack([s, r, c]).astype(jnp.int32)
    cmap = child_map.reshape(-1)
    tile_rows, tile_cols = parent_front.shape
    panel = child_panel[0]
    weights = jnp.repeat(child_pattern[0].astype(F32), B, axis=1)

    oct_rows = lax.dynamic_slice_in_dim(panel.reshape(8, 8, 32, K), c, 1, 1)[:, 0]
    oct_w = weights.reshape(8, 2, K)
    oct_w = jnp.where(c >= 4, oct_w[:, 1], oct_w[:, 0])
    outgoing = jnp.repeat(oct_rows * oct_w[:, None, :], 2, axis=0)
    q_half = lax.dynamic_slice_in_dim(panel, core * 64, 64, 0) * weights[0][None, :]
    outgoing = jnp.concatenate([outgoing, jnp.broadcast_to(q_half[None], (16, 64, K))], axis=1)
    arrived = lax.all_to_all(outgoing, ("sub", "row"), split_axis=0, concat_axis=0, tiled=True)

    slabs = parent_front[:, :PW].reshape(2, 8, 64, PW).transpose(1, 0, 2, 3).reshape(4, 2, B, PW)
    mate = permute(slabs[:, 1], move_pairs("k", 1, lambda s, r, c: c == 0))
    mine = jnp.where(core == 0, slabs[:, 0], mate)
    near_y = lambda s, r, c: c < 2
    share = jnp.where(y == 0, mine[0], jnp.zeros_like(mine[0]))
    for k in (1, 3, 2):
        share = share + permute(mine[k], move_pairs("y", k, near_y))

    slab = share[:64]
    at_root = (lambda s, r, c: s == 0 and r == 0)
    on_line = (lambda s, r, c: (s == 0) if c % 2 else (r == 0))

    def first_axis_is_root(s, r, c):
        return s == 0 and r == 0

    def second_axis_is_root(s, r, c):
        return r == 0 if axis_of(1, c) == "z" else s == 0

    here = jnp.where((s == 0) & (r == 0), slab, jnp.zeros_like(slab))
    one = here
    for k in (1, 3, 2):
        one = one + permute(here, pairs(0, k, first_axis_is_root))
    two = one
    for k in (1, 3, 2):
        two = two + permute(one, pairs(1, k, second_axis_is_root))
    ring_y = [two] + [permute(two, move_pairs("y", k)) for k in (1, 3, 2)]
    ring_y = jnp.stack([ring_y[0], ring_y[1], ring_y[2], ring_y[3]])
    corner = jnp.concatenate([ring_y, permute(ring_y, move_pairs("k", 1))], axis=0)

    arrived, corner = lax.optimization_barrier((arrived, corner))
    q_own = arrived[:, 32:]
    q_mate = permute(q_own, move_pairs("k", 1))
    row_share = jnp.concatenate([arrived[:, :32].reshape(16 * 32, K), share], axis=0)
    up_y = permute(row_share, move_pairs("y", 1))
    down_y = permute(row_share, move_pairs("y", -1))

    to_shard = []
    for g in range(16):
        for cc in range(8):
            b = 8 * g + cc
            to_shard.append((g * 8 + cc, (b % 16) * 8 + b // 16))
    panel_share = permute(share, to_shard)
    own_rows = lax.dynamic_slice_in_dim(panel, c * (E * B), E * B, 0).reshape(E, B, K)
    own_w = lax.dynamic_slice_in_dim(weights, c * E, E, 0)
    col_share = jnp.concatenate([(own_rows * own_w[:, None, :]).reshape(E * B, K), panel_share], axis=0)
    up, down = ring_near(col_share, 0)
    up, down, corner = lax.optimization_barrier((up, down, corner))
    line = stack_rows([col_share, up, down, *ring_far(up, down, 0)])
    line, corner = lax.optimization_barrier((line, corner))
    up, down = ring_near(line, 1)

    vmem = pl.BlockSpec(memory_space=pltpu.VMEM)
    smem = pl.BlockSpec(memory_space=pltpu.SMEM)
    half_done, upper, x_cat = pl.pallas_call(
        corner_kernel,
        in_specs=[smem, smem, vmem, vmem, vmem],
        out_specs=[vmem, vmem, vmem],
        out_shape=[
            jax.ShapeDtypeStruct((PW, PW), F32),
            jax.ShapeDtypeStruct((PW, PW), F32),
            jax.ShapeDtypeStruct((4, PW, 3 * K), BF16),
        ],
        scratch_shapes=[pltpu.VMEM((4, PW, 2 * K), BF16)],
        compiler_params=pltpu.CompilerParams(vmem_limit_bytes=40 * MIB),
        cost_estimate=pl.CostEstimate(flops=18_000_000_000, bytes_accessed=12 * MIB, transcendentals=0),
    )(idx, cmap, corner, q_own, q_mate)
    up_t, down_t, up_y, down_y, half_done = lax.optimization_barrier((up, down, up_y, down_y, half_done))
    far_a, far_b = ring_far(up_t, down_t, 1)
    far_y = (permute(up_y[:320], move_pairs("y", 1)), permute(down_y[320:], move_pairs("y", -1)))
    half_done, upper = pl.pallas_call(
        next_kernel,
        in_specs=[vmem, vmem],
        out_specs=[vmem, vmem],
        out_shape=[jax.ShapeDtypeStruct((PW, PW), F32), jax.ShapeDtypeStruct((PW, PW), F32)],
        compiler_params=pltpu.CompilerParams(vmem_limit_bytes=40 * MIB),
        cost_estimate=pl.CostEstimate(flops=12_000_000_000, bytes_accessed=4 * MIB, transcendentals=0),
    )(half_done, upper)
    far_y = lax.optimization_barrier((*far_y, half_done))
    far_y, half_done = far_y[:2], far_y[2]
    row_data = stack_rows([row_share, up_y, down_y, *far_y])
    row_data, half_done = lax.optimization_barrier((row_data, half_done))
    row_mate = permute(row_data, move_pairs("k", 1)).reshape(4, 640, K)
    row_data = row_data.reshape(4, 640, K)
    lower, lower_inv = pl.pallas_call(
        finish_kernel,
        in_specs=[vmem, vmem],
        out_specs=[vmem, vmem],
        out_shape=[
            jax.ShapeDtypeStruct((PW, PW), F32),
            jax.ShapeDtypeStruct((PW, 3 * PW), BF16),
        ],
        scratch_shapes=[pltpu.VMEM((PW, PW), F32), pltpu.VMEM((PW, PW), F32)],
        compiler_params=pltpu.CompilerParams(vmem_limit_bytes=40 * MIB),
        cost_estimate=pl.CostEstimate(flops=22_000_000_000, bytes_accessed=5 * MIB, transcendentals=0),
    )(half_done, upper)

    def child_rows(i, idx, cmap):
        return (0, (idx[0] + offset(i)) % 4, 0)

    hbm = pl.BlockSpec(memory_space=pltpu.HBM)
    once = pl.Buffered(1)
    schur, own = pl.pallas_call(
        tile_kernel,
        grid_spec=pltpu.PrefetchScalarGridSpec(
            num_scalar_prefetch=2,
            grid=(4,),
            in_specs=[
                pl.BlockSpec((4, B, K), child_rows),
                pl.BlockSpec((4, B, K), child_rows),
                pl.BlockSpec((4, B, K), lambda i, idx, cmap: (0, 4, 0), pipeline_mode=once),
                pl.BlockSpec((4, B, K), lambda i, idx, cmap: (0, 4, 0), pipeline_mode=once),
                pl.BlockSpec((1, PW, 3 * K), lambda i, idx, cmap: (i, 0, 0)),
                pl.BlockSpec((PW, PW), lambda i, idx, cmap: (0, 0), pipeline_mode=once),
                pl.BlockSpec((PW, 3 * PW), lambda i, idx, cmap: (0, 0), pipeline_mode=once),
            ]
            + [hbm] * 6,
            out_specs=[hbm, hbm],
            scratch_shapes=[
                pltpu.VMEM((tile_rows + B, tile_cols), F32),
                pltpu.VMEM((tile_rows + B, PW), F32),
                pltpu.VMEM((tile_cols, PW), F32),
                pltpu.VMEM((tile_rows, 3 * K), BF16),
                pltpu.VMEM((tile_rows, 3 * K), BF16),
                pltpu.VMEM((256, 3 * K), BF16),
                pltpu.VMEM((2, 4, 3 * B, K), F32),
                pltpu.SemaphoreType.DMA((3,)),
                pltpu.SemaphoreType.DMA((2, 4)),
            ],
        ),
        out_shape=[
            jax.ShapeDtypeStruct((tile_rows, tile_cols), F32),
            jax.ShapeDtypeStruct((tile_rows, PW), F32),
        ],
        compiler_params=pltpu.CompilerParams(
            vmem_limit_bytes=56 * MIB, dimension_semantics=("arbitrary",)
        ),
        cost_estimate=pl.CostEstimate(flops=45_000_000_000, bytes_accessed=50 * MIB, transcendentals=0),
    )(idx, cmap, row_data, row_mate, row_data, row_mate, x_cat, lower, lower_inv, line, up_t, down_t, far_a, far_b, parent_front)
    return schur, own


def solution(mesh):
    placed = (P(("sub", "row"), "col"), P("sub", "row", None), P("sub", "row", None), P())
    return jax.shard_map(
        per_device,
        mesh=mesh,
        in_specs=placed,
        out_specs=(P(("sub", "row"), "col"), P(("sub", "row"), None)),
        check_vma=False,
    )
```

```python
import functools

import jax
import jax.numpy as jnp
from jax import lax
from jax.experimental import pallas as pl
from jax.experimental.pallas import tpu as pltpu
from jax.sharding import PartitionSpec as P

B = 128
K = 512
E = 2
PW = 512
ALL = ("sub", "row", "col")
NS, NR, NC = 4, 4, 8
OFFS = (0, 3, 1, 2)
F32 = jnp.float32
BF16 = jnp.bfloat16
MIB = 1 << 20


def gid(s, r, c):
    return (s * NR + r) * NC + c


DEVICES = [(s, r, c) for s in range(NS) for r in range(NR) for c in range(NC)]


def moved(axis, k, s, r, c):
    if axis == "x":
        return ((s + k) % NS, r, c)
    if axis == "z":
        return (s, (r + k) % NR, c)
    if axis == "y":
        return (s, r, (c + 2 * k) % NC)
    return (s, r, c ^ 1)


def axis_of(phase, c):
    return "zx"[(phase + c % 2) % 2]


def pairs(phase, k, where=lambda s, r, c: True):
    return [
        (gid(s, r, c), gid(*moved(axis_of(phase, c), k, s, r, c)))
        for s, r, c in DEVICES
        if where(s, r, c)
    ]


def move_pairs(axis, k, where=lambda s, r, c: True):
    return [(gid(s, r, c), gid(*moved(axis, k, s, r, c))) for s, r, c in DEVICES if where(s, r, c)]


def permute(x, prs):
    return lax.ppermute(x, ALL, prs)


def ring_near(x, phase):
    return permute(x, pairs(phase, 1)), permute(x, pairs(phase, -1))


def ring_far(up, down, phase):
    half = up.shape[0] // 2
    return permute(up[:half], pairs(phase, 1)), permute(down[half:], pairs(phase, -1))


def split(x):
    hi = x.astype(BF16)
    lo = (x - hi.astype(F32)).astype(BF16)
    return hi, lo


def left_cat(x):
    hi, lo = split(x)
    return jnp.concatenate([hi, lo, hi], axis=1)


def right_cat(x):
    hi, lo = split(x)
    return jnp.concatenate([hi, hi, lo], axis=1)


def dot_t(a, b, precision=None):
    return lax.dot_general(
        a, b, (((1,), (1,)), ((), ())), precision=precision, preferred_element_type=F32
    )


def offset(p):
    return jnp.where(p == 0, 0, jnp.where(p == 1, 3, jnp.where(p == 2, 1, 2)))


def factor_block(rows):
    n = len(rows)
    w = list(rows)
    lane = lax.broadcasted_iota(jnp.int32, (8, B), 1)
    sub = lax.broadcasted_iota(jnp.int32, (8, B), 0)
    upper = [None] * n
    for j in range(0, B, 4):
        k0, o = j // 8, j % 8
        cols = [
            [jnp.broadcast_to(w[k][:, j + m : j + m + 1], (8, B)) for m in range(4)]
            for k in range(k0, n)
        ]
        top = cols[0]

        def elem(p, q):
            return jnp.broadcast_to(top[q][o + p : o + p + 1, :], (8, B))

        l = {}
        inv = [None] * 4
        for q in range(4):
            d = elem(q, q)
            for t in range(q):
                d = d - l[q, t] * l[q, t]
            inv[q] = lax.rsqrt(d)
            l[q, q] = d * inv[q]
            for p in range(q + 1, 4):
                e = elem(p, q)
                for t in range(q):
                    e = e - l[p, t] * l[q, t]
                l[p, q] = e * inv[q]
        in_block = (lane >= j) & (lane < j + 4)
        orig = [jnp.broadcast_to(w[k0][o + m : o + m + 1, :], (8, B)) for m in range(4)]
        ident = [
            jnp.where(in_block, jnp.where(lane == j + m, 1.0, 0.0).astype(F32), orig[m])
            for m in range(4)
        ]
        uo, ui = [], []
        for m in range(4):
            a, b = orig[m], ident[m]
            for t in range(m):
                a = a - l[m, t] * uo[t]
                b = b - l[m, t] * ui[t]
            uo.append(a * inv[m])
            ui.append(b * inv[m])
        back = [None] * 4
        for m in (3, 2, 1, 0):
            a = ui[m]
            for t in range(m + 1, 4):
                a = a - l[t, m] * back[t]
            back[m] = a * inv[m]
        acc_u = upper[k0] if upper[k0] is not None else jnp.zeros((8, B), F32)
        new_rows = w[k0]
        for m in range(4):
            at = sub == o + m
            acc_u = jnp.where(at & (lane >= j + m), uo[m], acc_u)
            new_rows = jnp.where(at, ui[m], new_rows)
        upper[k0] = acc_u
        for k in range(k0, n):
            if k == k0 and o == 4:
                w[k] = new_rows
                continue
            c = cols[k - k0]
            x = jnp.where(in_block, 0.0, w[k])
            x = x - (c[0] * back[0] + c[1] * back[1]) - (c[2] * back[2] + c[3] * back[3])
            w[k] = jnp.where(sub >= 4, x, new_rows) if k == k0 else x
    for k in range(n):
        w[k] = jnp.where(lane <= sub + 8 * k, w[k], 0.0)
    return upper, w


def factor_stage(b, w, ut):
    col = lax.broadcasted_iota(jnp.int32, (B, PW), 1)
    row = lax.broadcasted_iota(jnp.int32, (B, B), 0)
    col_b = lax.broadcasted_iota(jnp.int32, (B, B), 1)
    eye = jnp.where(row == col_b, 1.0, 0.0).astype(F32)
    o = b * B if isinstance(b, int) else pl.multiple_of(b * B, B)
    blk = pl.ds(o, B)
    diag = w[blk, blk]
    upper, inv = factor_block([diag[8 * k : 8 * k + 8, :] for k in range(16)])
    inv = jnp.concatenate(inv, axis=0)
    w[blk, blk] = eye
    u = jnp.dot(inv, w[blk, :], precision=lax.Precision.HIGHEST, preferred_element_type=F32)
    right = jnp.where(col >= o + B, u, 0.0)
    ut[blk, :] = right
    ut[blk, blk] = jnp.concatenate(upper, axis=0)
    w[:, blk] = jnp.zeros((PW, B), F32)
    w[...] -= lax.dot_general(
        right,
        u,
        (((0,), (0,)), ((), ())),
        precision=lax.Precision.HIGHEST,
        preferred_element_type=F32,
    )
    w[blk, :] = u


def corner_kernel(idx, cmap, corner, q_own, q_mate, w, ut, x_out, xs):
    s, r, c = idx[0], idx[1], idx[2]
    core = c % 2
    y = c // 2
    for kk in range(2):
        for p in range(4):
            at = 64 * (2 * ((y + OFFS[p]) % 4) + (core if kk == 0 else 1 - core))
            w[pl.ds(pl.multiple_of(at, 64), 64), :] = corner[kk * 4 + p]
    xs[...] = jnp.zeros_like(xs)
    ut[...] = jnp.zeros_like(ut)
    for i in range(4):
        child = (s + OFFS[i]) % 4
        for row in range(4):
            slot = cmap[child * 64 + row * 16]

            @pl.when(slot < 4)
            def _():
                for half, ref in ((core, q_own), (1 - core, q_mate)):
                    hi, lo = split(ref[child * 4 + row, 32:96, :])
                    at = pl.ds(pl.multiple_of(slot * B + half * 64, 64), 64)
                    xs[i, at, 0:K] = hi
                    xs[i, at, K : 2 * K] = lo
    for i in range(4):
        hi, lo = xs[i, :, 0:K], xs[i, :, K : 2 * K]
        x_out[i, :, 0:K] = hi
        x_out[i, :, K : 2 * K] = hi
        x_out[i, :, 2 * K :] = lo
        a = jnp.concatenate([hi, lo, hi], axis=1)
        b = jnp.concatenate([hi, hi, lo], axis=1)
        w[...] -= dot_t(a, b)

    factor_stage(0, w, ut)


def next_kernel(stage, w_in, ut_in, w, ut):
    w[...] = w_in[...]
    ut[...] = ut_in[...]
    factor_stage(stage, w, ut)


def middle_stage(stage, w, ut):
    vmem = pl.BlockSpec(memory_space=pltpu.VMEM)
    return pl.pallas_call(
        functools.partial(next_kernel, stage),
        in_specs=[vmem, vmem],
        out_specs=[vmem, vmem],
        out_shape=[jax.ShapeDtypeStruct((PW, PW), F32), jax.ShapeDtypeStruct((PW, PW), F32)],
        compiler_params=pltpu.CompilerParams(vmem_limit_bytes=40 * MIB),
        cost_estimate=pl.CostEstimate(flops=11_000_000_000, bytes_accessed=4 * MIB, transcendentals=0),
    )(w, ut)


def stack_kernel(*refs):
    pieces, out, sem = refs[:-2], refs[-2], refs[-1]
    copies = []
    at = 0
    for k, piece in enumerate(pieces):
        rows = piece.shape[0]
        copies.append(pltpu.make_async_copy(piece, out.at[pl.ds(at, rows), :], sem.at[k]))
        copies[-1].start()
        at += rows
    for copy in copies:
        copy.wait()


def stack_rows(pieces):
    hbm = pl.BlockSpec(memory_space=pltpu.HBM)
    rows = sum(x.shape[0] for x in pieces)
    width = pieces[0].shape[1]
    return pl.pallas_call(
        stack_kernel,
        in_specs=[hbm] * len(pieces),
        out_specs=pl.BlockSpec(memory_space=pltpu.VMEM),
        out_shape=jax.ShapeDtypeStruct((rows, width), F32),
        compiler_params=pltpu.CompilerParams(vmem_limit_bytes=16 * MIB),
        scratch_shapes=[pltpu.SemaphoreType.DMA((len(pieces),))],
        cost_estimate=pl.CostEstimate(flops=0, bytes_accessed=8 * rows * width, transcendentals=0),
    )(*pieces)


def finish_kernel(w_in, ut_in, l_out, li_out, w, ut):
    w[...] = w_in[...]
    ut[...] = ut_in[...]

    factor_stage(3, w, ut)
    rows = lax.broadcasted_iota(jnp.int32, (PW, PW), 0)
    cols = lax.broadcasted_iota(jnp.int32, (PW, PW), 1)
    li_out[...] = right_cat(jnp.where(cols <= rows, w[...], 0.0))
    l_out[...] = ut[...].T


def tile_kernel(
    idx, cmap, rows_a, rows_b, pg_a, pg_b, x_ref, l_ref, li_ref, c0, c1, c2, c3a, c3b, parent, out, own_out,
    acc, pg, pc, rcat, ocat, fcat, sbuf, sem, ssem,
):
    s, r, c = idx[0], idx[1], idx[2]
    core = c % 2
    group = s * 4 + r
    i = pl.program_id(0)
    tile_rows, tile_cols = parent.shape
    load = pltpu.make_async_copy(parent, acc.at[pl.ds(0, tile_rows), :], sem.at[0])
    slot = lax.rem(i, 2)
    y = c // 2

    def octant(kk, p):
        return 2 * ((y + OFFS[p]) % 4) + (core if kk == 0 else 1 - core)

    def chunk(piece, n):
        ref = (c0, c1, c2, (c3a, c3b)[n // 2])[piece]
        n = n % 2 if piece == 3 else n
        return ref.at[pl.ds(3 * B * n, 3 * B), :]

    def fetch(step):
        for n in range(4):

            @pl.when(step == n)
            def _():
                @pl.when(core == 0)
                def _():
                    for j in range(4):
                        pltpu.make_async_copy(chunk(n, j), sbuf.at[n % 2, j], ssem.at[n % 2, j]).start()

                @pl.when(core == 1)
                def _():
                    for j in range(4):
                        pltpu.make_async_copy(chunk(j, n), sbuf.at[n % 2, j], ssem.at[n % 2, j]).start()

    @pl.when(i == 0)
    def _():
        fetch(i)
        load.start()
        pc[...] = jnp.zeros_like(pc)
        for kk, ref in ((0, pg_a), (1, pg_b)):
            for p in range(4):
                at = 64 * octant(kk, p)
                pg[pl.ds(pl.multiple_of(at, 64), 64), :] = ref[p, 0:64, :]
                pg[pl.ds(pl.multiple_of(at + 512, 64), 64), :] = ref[p, 64:128, :]

    fetch(i + 1)
    child = (s + offset(i)) % 4
    for kk, ref in ((0, rows_a), (1, rows_b)):
        for p in range(4):
            o = octant(kk, p)
            part = left_cat(ref[p])
            for rr in range(4):
                at = pl.multiple_of((2 * rr + o // 4) * B + 32 * (o % 4), 32)
                rcat[pl.ds(at, 32), :] = part[32 * rr : 32 * rr + 32, :]
    x = x_ref[0]

    def row_slot(rr, e):
        v = cmap[child * 64 + rr * 16 + (group // 2) * 2 + e] - group * 8
        return jnp.where((v >= 0) & (v < 8), v, 8)

    places = [pl.multiple_of(row_slot(rr, e) * B, B) for rr in range(4) for e in range(2)]

    def to_rows(dst, value, cols):
        for n, at in enumerate(places):
            dst[pl.ds(at, B), cols] -= value[B * n : B * n + B, :]

    for h in range(2):
        cols = slice(256 * h, 256 * h + 256)
        to_rows(pg, dot_t(rcat[...], x_ref[0, cols, :]), cols)

    @pl.when(i == 0)
    def _():
        load.wait()

    for j in range(4):
        pltpu.make_async_copy(chunk(0, 0), sbuf.at[slot, j], ssem.at[slot, j]).wait()

    for j in range(4):
        piece = sbuf.at[slot, pl.ds(j, 1)]
        rr = (r + OFFS[j]) % 4
        shard = child * 4 + rr
        at = (shard // 8) * 1024 + 64 * (shard % 8)
        pc[pl.ds(pl.multiple_of(at, 64), 64), :] += piece[0, 256:320, :]
        pc[pl.ds(pl.multiple_of(at + 512, 64), 64), :] += piece[0, 320:384, :]
        hi, lo = split(piece[0, 0:256, :])
        scat = jnp.concatenate([hi, hi, lo], axis=1)
        prod = dot_t(rcat[...], scat)
        up = dot_t(jnp.concatenate([hi, lo, hi], axis=1), x)
        for e in range(2):
            place = cmap[child * 64 + rr * 16 + c * 2 + e] - c * 16
            at = pl.multiple_of(place * B, B)
            pc[pl.ds(at, B), :] -= up[B * e : B * e + B, :]
            to_rows(acc, prod[:, B * e : B * e + B], pl.ds(at, B))

    @pl.when(i == 3)
    def _():
        li = li_ref[...]
        own = dot_t(left_cat(pg[pl.ds(0, tile_rows), :]), li)
        pg[pl.ds(0, tile_rows), :] = own

        @pl.when(group == 0)
        def _():
            pg[pl.ds(0, PW), :] = l_ref[...]

        ocat[...] = left_cat(pg[pl.ds(0, tile_rows), :])
        send_own = pltpu.make_async_copy(pg.at[pl.ds(0, tile_rows), :], own_out, sem.at[1])
        send_own.start()
        for n in range(tile_cols // 256):
            cols = pl.ds(256 * n, 256)
            far = dot_t(left_cat(pc[cols, :]), li)
            if n < 2:
                far = jnp.where(c == 0, l_ref[cols, :], far)
            fcat[...] = right_cat(far)
            acc[pl.ds(0, tile_rows), cols] -= dot_t(ocat[...], fcat[...])
            pltpu.make_async_copy(
                acc.at[pl.ds(0, tile_rows), cols], out.at[:, cols], sem.at[2]
            ).start()
        pltpu.make_async_copy(acc.at[pl.ds(0, tile_rows), :], out, sem.at[2]).wait()
        send_own.wait()


def per_device(parent_front, child_panel, child_pattern, child_map):
    s = lax.axis_index("sub")
    r = lax.axis_index("row")
    c = lax.axis_index("col")
    y, core = c // 2, c % 2
    idx = jnp.stack([s, r, c]).astype(jnp.int32)
    cmap = child_map.reshape(-1)
    tile_rows, tile_cols = parent_front.shape
    panel = child_panel[0]
    weights = jnp.repeat(child_pattern[0].astype(F32), B, axis=1)

    oct_rows = lax.dynamic_slice_in_dim(panel.reshape(8, 8, 32, K), c, 1, 1)[:, 0]
    oct_w = weights.reshape(8, 2, K)
    oct_w = jnp.where(c >= 4, oct_w[:, 1], oct_w[:, 0])
    outgoing = jnp.repeat(oct_rows * oct_w[:, None, :], 2, axis=0)
    q_half = lax.dynamic_slice_in_dim(panel, core * 64, 64, 0) * weights[0][None, :]
    outgoing = jnp.concatenate([outgoing, jnp.broadcast_to(q_half[None], (16, 64, K))], axis=1)
    arrived = lax.all_to_all(outgoing, ("sub", "row"), split_axis=0, concat_axis=0, tiled=True)

    slabs = parent_front[:, :PW].reshape(2, 8, 64, PW).transpose(1, 0, 2, 3).reshape(4, 2, B, PW)
    mate = permute(slabs[:, 1], move_pairs("k", 1, lambda s, r, c: c == 0))
    mine = jnp.where(core == 0, slabs[:, 0], mate)
    near_y = lambda s, r, c: c < 2
    share = jnp.where(y == 0, mine[0], jnp.zeros_like(mine[0]))
    for k in (1, 3, 2):
        share = share + permute(mine[k], move_pairs("y", k, near_y))

    slab = share[:64]
    at_root = (lambda s, r, c: s == 0 and r == 0)
    on_line = (lambda s, r, c: (s == 0) if c % 2 else (r == 0))

    def first_axis_is_root(s, r, c):
        return s == 0 and r == 0

    def second_axis_is_root(s, r, c):
        return r == 0 if axis_of(1, c) == "z" else s == 0

    here = jnp.where((s == 0) & (r == 0), slab, jnp.zeros_like(slab))
    one = here
    for k in (1, 3, 2):
        one = one + permute(here, pairs(0, k, first_axis_is_root))
    two = one
    for k in (1, 3, 2):
        two = two + permute(one, pairs(1, k, second_axis_is_root))
    to_shard = []
    for g in range(16):
        for cc in range(8):
            b = 8 * g + cc
            to_shard.append((g * 8 + cc, (b % 16) * 8 + b // 16))
    panel_share = permute(share, to_shard)
    own_rows = lax.dynamic_slice_in_dim(panel, c * (E * B), E * B, 0).reshape(E, B, K)
    own_w = lax.dynamic_slice_in_dim(weights, c * E, E, 0)
    col_share = jnp.concatenate([(own_rows * own_w[:, None, :]).reshape(E * B, K), panel_share], axis=0)
    col_share, two = lax.optimization_barrier((col_share, two))
    up, down = ring_near(col_share, 0)
    ring_y = [two] + [permute(two, move_pairs("y", k)) for k in (1, 3, 2)]
    ring_y = jnp.stack([ring_y[0], ring_y[1], ring_y[2], ring_y[3]])
    ring_y, up, down = lax.optimization_barrier((ring_y, up, down))
    line = stack_rows([col_share, up, down, *ring_far(up, down, 0)])
    corner = jnp.concatenate([ring_y, permute(ring_y, move_pairs("k", 1))], axis=0)

    arrived, corner = lax.optimization_barrier((arrived, corner))
    arrived_mate = permute(arrived, move_pairs("k", 1))
    row_share = jnp.concatenate([arrived[:, :32].reshape(16 * 32, K), share], axis=0)
    up_y = permute(row_share, move_pairs("y", 1))
    down_y = permute(row_share, move_pairs("y", -1))

    line, corner = lax.optimization_barrier((line, corner))
    up, down = ring_near(line, 1)

    vmem = pl.BlockSpec(memory_space=pltpu.VMEM)
    smem = pl.BlockSpec(memory_space=pltpu.SMEM)
    half_done, upper, x_cat = pl.pallas_call(
        corner_kernel,
        in_specs=[smem, smem, vmem, vmem, vmem],
        out_specs=[vmem, vmem, vmem],
        out_shape=[
            jax.ShapeDtypeStruct((PW, PW), F32),
            jax.ShapeDtypeStruct((PW, PW), F32),
            jax.ShapeDtypeStruct((4, PW, 3 * K), BF16),
        ],
        scratch_shapes=[pltpu.VMEM((4, PW, 2 * K), BF16)],
        compiler_params=pltpu.CompilerParams(vmem_limit_bytes=40 * MIB),
        cost_estimate=pl.CostEstimate(flops=18_000_000_000, bytes_accessed=12 * MIB, transcendentals=0),
    )(idx, cmap, corner, arrived, arrived_mate)
    half_done, upper = middle_stage(1, half_done, upper)
    up_t, down_t, up_y, down_y, half_done = lax.optimization_barrier((up, down, up_y, down_y, half_done))
    far_a, far_b = ring_far(up_t, down_t, 1)
    far_y = (permute(up_y[:320], move_pairs("y", 1)), permute(down_y[320:], move_pairs("y", -1)))
    half_done, upper = middle_stage(2, half_done, upper)
    *far_y, far_a, far_b, half_done = lax.optimization_barrier((*far_y, far_a, far_b, half_done))
    row_data = stack_rows([row_share, up_y, down_y, *far_y])
    row_data, half_done = lax.optimization_barrier((row_data, half_done))
    row_mate = permute(row_data, move_pairs("k", 1)).reshape(4, 640, K)
    row_data = row_data.reshape(4, 640, K)
    lower, lower_inv = pl.pallas_call(
        finish_kernel,
        in_specs=[vmem, vmem],
        out_specs=[vmem, vmem],
        out_shape=[
            jax.ShapeDtypeStruct((PW, PW), F32),
            jax.ShapeDtypeStruct((PW, 3 * PW), BF16),
        ],
        scratch_shapes=[pltpu.VMEM((PW, PW), F32), pltpu.VMEM((PW, PW), F32)],
        compiler_params=pltpu.CompilerParams(vmem_limit_bytes=40 * MIB),
        cost_estimate=pl.CostEstimate(flops=12_000_000_000, bytes_accessed=5 * MIB, transcendentals=0),
    )(half_done, upper)

    def child_rows(i, idx, cmap):
        return (0, (idx[0] + offset(i)) % 4, 0)

    hbm = pl.BlockSpec(memory_space=pltpu.HBM)
    once = pl.Buffered(1)
    schur, own = pl.pallas_call(
        tile_kernel,
        grid_spec=pltpu.PrefetchScalarGridSpec(
            num_scalar_prefetch=2,
            grid=(4,),
            in_specs=[
                pl.BlockSpec((4, B, K), child_rows),
                pl.BlockSpec((4, B, K), child_rows),
                pl.BlockSpec((4, B, K), lambda i, idx, cmap: (0, 4, 0), pipeline_mode=once),
                pl.BlockSpec((4, B, K), lambda i, idx, cmap: (0, 4, 0), pipeline_mode=once),
                pl.BlockSpec((1, PW, 3 * K), lambda i, idx, cmap: (i, 0, 0)),
                pl.BlockSpec((PW, PW), lambda i, idx, cmap: (0, 0), pipeline_mode=once),
                pl.BlockSpec((PW, 3 * PW), lambda i, idx, cmap: (0, 0), pipeline_mode=once),
            ]
            + [hbm] * 6,
            out_specs=[hbm, hbm],
            scratch_shapes=[
                pltpu.VMEM((tile_rows + B, tile_cols), F32),
                pltpu.VMEM((tile_rows + B, PW), F32),
                pltpu.VMEM((tile_cols, PW), F32),
                pltpu.VMEM((tile_rows, 3 * K), BF16),
                pltpu.VMEM((tile_rows, 3 * K), BF16),
                pltpu.VMEM((256, 3 * K), BF16),
                pltpu.VMEM((2, 4, 3 * B, K), F32),
                pltpu.SemaphoreType.DMA((3,)),
                pltpu.SemaphoreType.DMA((2, 4)),
            ],
        ),
        out_shape=[
            jax.ShapeDtypeStruct((tile_rows, tile_cols), F32),
            jax.ShapeDtypeStruct((tile_rows, PW), F32),
        ],
        compiler_params=pltpu.CompilerParams(
            vmem_limit_bytes=56 * MIB, dimension_semantics=("arbitrary",)
        ),
        cost_estimate=pl.CostEstimate(flops=45_000_000_000, bytes_accessed=50 * MIB, transcendentals=0),
    )(idx, cmap, row_data, row_mate, row_data, row_mate, x_cat, lower, lower_inv, line, up_t, down_t, far_a, far_b, parent_front)
    return schur, own


def solution(mesh):
    placed = (P(("sub", "row"), "col"), P("sub", "row", None), P("sub", "row", None), P())
    return jax.shard_map(
        per_device,
        mesh=mesh,
        in_specs=placed,
        out_specs=(P(("sub", "row"), "col"), P(("sub", "row"), None)),
        check_vma=False,
    )
```

```python
import functools

import jax
import jax.numpy as jnp
from jax import lax
from jax.experimental import pallas as pl
from jax.experimental.pallas import tpu as pltpu
from jax.sharding import PartitionSpec as P

B = 128
K = 512
E = 2
PW = 512
ALL = ("sub", "row", "col")
NS, NR, NC = 4, 4, 8
OFFS = (0, 3, 1, 2)
F32 = jnp.float32
BF16 = jnp.bfloat16
MIB = 1 << 20


def gid(s, r, c):
    return (s * NR + r) * NC + c


DEVICES = [(s, r, c) for s in range(NS) for r in range(NR) for c in range(NC)]


def moved(axis, k, s, r, c):
    if axis == "x":
        return ((s + k) % NS, r, c)
    if axis == "z":
        return (s, (r + k) % NR, c)
    if axis == "y":
        return (s, r, (c + 2 * k) % NC)
    return (s, r, c ^ 1)


def axis_of(phase, c):
    return "zx"[(phase + c % 2) % 2]


def pairs(phase, k, where=lambda s, r, c: True):
    return [
        (gid(s, r, c), gid(*moved(axis_of(phase, c), k, s, r, c)))
        for s, r, c in DEVICES
        if where(s, r, c)
    ]


def move_pairs(axis, k, where=lambda s, r, c: True):
    return [(gid(s, r, c), gid(*moved(axis, k, s, r, c))) for s, r, c in DEVICES if where(s, r, c)]


def permute(x, prs):
    return lax.ppermute(x, ALL, prs)


def ring_near(x, phase):
    return permute(x, pairs(phase, 1)), permute(x, pairs(phase, -1))


def ring_far(up, down, phase):
    half = up.shape[0] // 2
    return permute(up[:half], pairs(phase, 1)), permute(down[half:], pairs(phase, -1))


def split(x):
    hi = x.astype(BF16)
    lo = (x - hi.astype(F32)).astype(BF16)
    return hi, lo


def left_cat(x):
    hi, lo = split(x)
    return jnp.concatenate([hi, lo, hi], axis=1)


def right_cat(x):
    hi, lo = split(x)
    return jnp.concatenate([hi, hi, lo], axis=1)


def dot_t(a, b, precision=None):
    return lax.dot_general(
        a, b, (((1,), (1,)), ((), ())), precision=precision, preferred_element_type=F32
    )


def offset(p):
    return jnp.where(p == 0, 0, jnp.where(p == 1, 3, jnp.where(p == 2, 1, 2)))


def factor_block(rows):
    n = len(rows)
    w = list(rows)
    lane = lax.broadcasted_iota(jnp.int32, (8, B), 1)
    sub = lax.broadcasted_iota(jnp.int32, (8, B), 0)
    upper = [None] * n
    for j in range(0, B, 4):
        k0, o = j // 8, j % 8
        cols = [
            [jnp.broadcast_to(w[k][:, j + m : j + m + 1], (8, B)) for m in range(4)]
            for k in range(k0, n)
        ]
        top = cols[0]

        def elem(p, q):
            return jnp.broadcast_to(top[q][o + p : o + p + 1, :], (8, B))

        l = {}
        inv = [None] * 4
        for q in range(4):
            d = elem(q, q)
            for t in range(q):
                d = d - l[q, t] * l[q, t]
            inv[q] = lax.rsqrt(d)
            l[q, q] = d * inv[q]
            for p in range(q + 1, 4):
                e = elem(p, q)
                for t in range(q):
                    e = e - l[p, t] * l[q, t]
                l[p, q] = e * inv[q]
        in_block = (lane >= j) & (lane < j + 4)
        orig = [jnp.broadcast_to(w[k0][o + m : o + m + 1, :], (8, B)) for m in range(4)]
        ident = [
            jnp.where(in_block, jnp.where(lane == j + m, 1.0, 0.0).astype(F32), orig[m])
            for m in range(4)
        ]
        uo, ui = [], []
        for m in range(4):
            a, b = orig[m], ident[m]
            for t in range(m):
                a = a - l[m, t] * uo[t]
                b = b - l[m, t] * ui[t]
            uo.append(a * inv[m])
            ui.append(b * inv[m])
        back = [None] * 4
        for m in (3, 2, 1, 0):
            a = ui[m]
            for t in range(m + 1, 4):
                a = a - l[t, m] * back[t]
            back[m] = a * inv[m]
        acc_u = upper[k0] if upper[k0] is not None else jnp.zeros((8, B), F32)
        new_rows = w[k0]
        for m in range(4):
            at = sub == o + m
            acc_u = jnp.where(at & (lane >= j + m), uo[m], acc_u)
            new_rows = jnp.where(at, ui[m], new_rows)
        upper[k0] = acc_u
        for k in range(k0, n):
            if k == k0 and o == 4:
                w[k] = new_rows
                continue
            c = cols[k - k0]
            x = jnp.where(in_block, 0.0, w[k])
            x = x - (c[0] * back[0] + c[1] * back[1]) - (c[2] * back[2] + c[3] * back[3])
            w[k] = jnp.where(sub >= 4, x, new_rows) if k == k0 else x
    for k in range(n):
        w[k] = jnp.where(lane <= sub + 8 * k, w[k], 0.0)
    return upper, w


def factor_stage(b, w, ut):
    col = lax.broadcasted_iota(jnp.int32, (B, PW), 1)
    row = lax.broadcasted_iota(jnp.int32, (B, B), 0)
    col_b = lax.broadcasted_iota(jnp.int32, (B, B), 1)
    eye = jnp.where(row == col_b, 1.0, 0.0).astype(F32)
    o = b * B if isinstance(b, int) else pl.multiple_of(b * B, B)
    blk = pl.ds(o, B)
    diag = w[blk, blk]
    upper, inv = factor_block([diag[8 * k : 8 * k + 8, :] for k in range(16)])
    inv = jnp.concatenate(inv, axis=0)
    w[blk, blk] = eye
    u = jnp.dot(inv, w[blk, :], precision=lax.Precision.HIGHEST, preferred_element_type=F32)
    right = jnp.where(col >= o + B, u, 0.0)
    ut[blk, :] = right
    ut[blk, blk] = jnp.concatenate(upper, axis=0)
    w[:, blk] = jnp.zeros((PW, B), F32)
    w[...] -= lax.dot_general(
        right,
        u,
        (((0,), (0,)), ((), ())),
        precision=lax.Precision.HIGHEST,
        preferred_element_type=F32,
    )
    w[blk, :] = u


def corner_kernel(idx, cmap, corner, q_own, q_mate, w, ut, x_out, xs):
    s, r, c = idx[0], idx[1], idx[2]
    core = c % 2
    y = c // 2
    for kk in range(2):
        for p in range(4):
            at = 64 * (2 * ((y + OFFS[p]) % 4) + (core if kk == 0 else 1 - core))
            w[pl.ds(pl.multiple_of(at, 64), 64), :] = corner[kk * 4 + p]
    xs[...] = jnp.zeros_like(xs)
    ut[...] = jnp.zeros_like(ut)
    for i in range(4):
        child = (s + OFFS[i]) % 4
        for row in range(4):
            slot = cmap[child * 64 + row * 16]

            @pl.when(slot < 4)
            def _():
                for half, ref in ((core, q_own), (1 - core, q_mate)):
                    hi, lo = split(ref[child * 4 + row])
                    at = pl.ds(pl.multiple_of(slot * B + half * 64, 64), 64)
                    xs[i, at, 0:K] = hi
                    xs[i, at, K : 2 * K] = lo
    for i in range(4):
        hi, lo = xs[i, :, 0:K], xs[i, :, K : 2 * K]
        x_out[i, :, 0:K] = hi
        x_out[i, :, K : 2 * K] = hi
        x_out[i, :, 2 * K :] = lo
        a = jnp.concatenate([hi, lo, hi], axis=1)
        b = jnp.concatenate([hi, hi, lo], axis=1)
        w[...] -= dot_t(a, b)

    factor_stage(0, w, ut)


def next_kernel(stage, w_in, ut_in, w, ut):
    w[...] = w_in[...]
    ut[...] = ut_in[...]
    factor_stage(stage, w, ut)


def middle_stage(stage, w, ut):
    vmem = pl.BlockSpec(memory_space=pltpu.VMEM)
    return pl.pallas_call(
        functools.partial(next_kernel, stage),
        in_specs=[vmem, vmem],
        out_specs=[vmem, vmem],
        out_shape=[jax.ShapeDtypeStruct((PW, PW), F32), jax.ShapeDtypeStruct((PW, PW), F32)],
        compiler_params=pltpu.CompilerParams(vmem_limit_bytes=40 * MIB),
        cost_estimate=pl.CostEstimate(flops=11_000_000_000, bytes_accessed=4 * MIB, transcendentals=0),
    )(w, ut)


def stack_kernel(*refs):
    pieces, out, sem = refs[:-2], refs[-2], refs[-1]
    copies = []
    at = 0
    for k, piece in enumerate(pieces):
        rows = piece.shape[0]
        copies.append(pltpu.make_async_copy(piece, out.at[pl.ds(at, rows), :], sem.at[k]))
        copies[-1].start()
        at += rows
    for copy in copies:
        copy.wait()


def stack_rows(pieces):
    hbm = pl.BlockSpec(memory_space=pltpu.HBM)
    rows = sum(x.shape[0] for x in pieces)
    width = pieces[0].shape[1]
    return pl.pallas_call(
        stack_kernel,
        in_specs=[hbm] * len(pieces),
        out_specs=pl.BlockSpec(memory_space=pltpu.VMEM),
        out_shape=jax.ShapeDtypeStruct((rows, width), F32),
        compiler_params=pltpu.CompilerParams(vmem_limit_bytes=16 * MIB),
        scratch_shapes=[pltpu.SemaphoreType.DMA((len(pieces),))],
        cost_estimate=pl.CostEstimate(flops=0, bytes_accessed=8 * rows * width, transcendentals=0),
    )(*pieces)


def finish_kernel(w_in, ut_in, l_out, li_out, w, ut):
    w[...] = w_in[...]
    ut[...] = ut_in[...]

    factor_stage(3, w, ut)
    rows = lax.broadcasted_iota(jnp.int32, (PW, PW), 0)
    cols = lax.broadcasted_iota(jnp.int32, (PW, PW), 1)
    li_out[...] = right_cat(jnp.where(cols <= rows, w[...], 0.0))
    l_out[...] = ut[...].T


def tile_kernel(
    idx, cmap, rows_a, rows_b, pg_a, pg_b, x_ref, l_ref, li_ref, c0, c1, c2, c3a, c3b, parent, out, own_out,
    acc, pg, pc, rcat, ocat, fcat, sbuf, sem, ssem,
):
    s, r, c = idx[0], idx[1], idx[2]
    core = c % 2
    group = s * 4 + r
    i = pl.program_id(0)
    tile_rows, tile_cols = parent.shape
    load = pltpu.make_async_copy(parent, acc.at[pl.ds(0, tile_rows), :], sem.at[0])
    slot = lax.rem(i, 2)
    y = c // 2

    def octant(kk, p):
        return 2 * ((y + OFFS[p]) % 4) + (core if kk == 0 else 1 - core)

    def chunk(piece, n):
        ref = (c0, c1, c2, (c3a, c3b)[n // 2])[piece]
        n = n % 2 if piece == 3 else n
        return ref.at[pl.ds(3 * B * n, 3 * B), :]

    def fetch(step):
        for n in range(4):

            @pl.when(step == n)
            def _():
                @pl.when(core == 0)
                def _():
                    for j in range(4):
                        pltpu.make_async_copy(chunk(n, j), sbuf.at[n % 2, j], ssem.at[n % 2, j]).start()

                @pl.when(core == 1)
                def _():
                    for j in range(4):
                        pltpu.make_async_copy(chunk(j, n), sbuf.at[n % 2, j], ssem.at[n % 2, j]).start()

    @pl.when(i == 0)
    def _():
        fetch(i)
        load.start()
        pc[...] = jnp.zeros_like(pc)
        for kk, ref in ((0, pg_a), (1, pg_b)):
            for p in range(4):
                at = 64 * octant(kk, p)
                pg[pl.ds(pl.multiple_of(at, 64), 64), :] = ref[p, 0:64, :]
                pg[pl.ds(pl.multiple_of(at + 512, 64), 64), :] = ref[p, 64:128, :]

    fetch(i + 1)
    child = (s + offset(i)) % 4
    for kk, ref in ((0, rows_a), (1, rows_b)):
        for p in range(4):
            o = octant(kk, p)
            part = left_cat(ref[p])
            for rr in range(4):
                at = pl.multiple_of((2 * rr + o // 4) * B + 32 * (o % 4), 32)
                rcat[pl.ds(at, 32), :] = part[32 * rr : 32 * rr + 32, :]
    x = x_ref[0]

    def row_slot(rr, e):
        v = cmap[child * 64 + rr * 16 + (group // 2) * 2 + e] - group * 8
        return jnp.where((v >= 0) & (v < 8), v, 8)

    places = [pl.multiple_of(row_slot(rr, e) * B, B) for rr in range(4) for e in range(2)]

    def to_rows(dst, value, cols):
        for n, at in enumerate(places):
            dst[pl.ds(at, B), cols] -= value[B * n : B * n + B, :]

    for h in range(2):
        cols = slice(256 * h, 256 * h + 256)
        to_rows(pg, dot_t(rcat[...], x_ref[0, cols, :]), cols)

    @pl.when(i == 0)
    def _():
        load.wait()

    for j in range(4):
        pltpu.make_async_copy(chunk(0, 0), sbuf.at[slot, j], ssem.at[slot, j]).wait()

    for j in range(4):
        piece = sbuf.at[slot, pl.ds(j, 1)]
        rr = (r + OFFS[j]) % 4
        shard = child * 4 + rr
        at = (shard // 8) * 1024 + 64 * (shard % 8)
        pc[pl.ds(pl.multiple_of(at, 64), 64), :] += piece[0, 256:320, :]
        pc[pl.ds(pl.multiple_of(at + 512, 64), 64), :] += piece[0, 320:384, :]
        hi, lo = split(piece[0, 0:256, :])
        scat = jnp.concatenate([hi, hi, lo], axis=1)
        prod = dot_t(rcat[...], scat)
        up = dot_t(jnp.concatenate([hi, lo, hi], axis=1), x)
        for e in range(2):
            place = cmap[child * 64 + rr * 16 + c * 2 + e] - c * 16
            at = pl.multiple_of(place * B, B)
            pc[pl.ds(at, B), :] -= up[B * e : B * e + B, :]
            to_rows(acc, prod[:, B * e : B * e + B], pl.ds(at, B))

    @pl.when(i == 3)
    def _():
        li = li_ref[...]
        own = dot_t(left_cat(pg[pl.ds(0, tile_rows), :]), li)
        pg[pl.ds(0, tile_rows), :] = own

        @pl.when(group == 0)
        def _():
            pg[pl.ds(0, PW), :] = l_ref[...]

        ocat[...] = left_cat(pg[pl.ds(0, tile_rows), :])
        send_own = pltpu.make_async_copy(pg.at[pl.ds(0, tile_rows), :], own_out, sem.at[1])
        send_own.start()
        for n in range(tile_cols // 256):
            cols = pl.ds(256 * n, 256)
            far = dot_t(left_cat(pc[cols, :]), li)
            if n < 2:
                far = jnp.where(c == 0, l_ref[cols, :], far)
            fcat[...] = right_cat(far)
            acc[pl.ds(0, tile_rows), cols] -= dot_t(ocat[...], fcat[...])
            pltpu.make_async_copy(
                acc.at[pl.ds(0, tile_rows), cols], out.at[:, cols], sem.at[2]
            ).start()
        pltpu.make_async_copy(acc.at[pl.ds(0, tile_rows), :], out, sem.at[2]).wait()
        send_own.wait()


def per_device(parent_front, child_panel, child_pattern, child_map):
    s = lax.axis_index("sub")
    r = lax.axis_index("row")
    c = lax.axis_index("col")
    y, core = c // 2, c % 2
    idx = jnp.stack([s, r, c]).astype(jnp.int32)
    cmap = child_map.reshape(-1)
    tile_rows, tile_cols = parent_front.shape
    panel = child_panel[0]
    weights = jnp.repeat(child_pattern[0].astype(F32), B, axis=1)

    oct_rows = lax.dynamic_slice_in_dim(panel.reshape(8, 8, 32, K), c, 1, 1)[:, 0]
    oct_w = weights.reshape(8, 2, K)
    oct_w = jnp.where(c >= 4, oct_w[:, 1], oct_w[:, 0])
    outgoing = jnp.repeat(oct_rows * oct_w[:, None, :], 2, axis=0)
    q_half = lax.dynamic_slice_in_dim(panel, core * 64, 64, 0) * weights[0][None, :]
    outgoing = jnp.concatenate([outgoing, jnp.broadcast_to(q_half[None], (16, 64, K))], axis=1)
    arrived = lax.all_to_all(outgoing, ("sub", "row"), split_axis=0, concat_axis=0, tiled=True)

    slabs = parent_front[:, :PW].reshape(2, 8, 64, PW).transpose(1, 0, 2, 3).reshape(4, 2, B, PW)
    mate = permute(slabs[:, 1], move_pairs("k", 1, lambda s, r, c: c == 0))
    mine = jnp.where(core == 0, slabs[:, 0], mate)
    near_y = lambda s, r, c: c < 2
    share = jnp.where(y == 0, mine[0], jnp.zeros_like(mine[0]))
    for k in (1, 3, 2):
        share = share + permute(mine[k], move_pairs("y", k, near_y))

    slab = share[:64]
    at_root = (lambda s, r, c: s == 0 and r == 0)
    on_line = (lambda s, r, c: (s == 0) if c % 2 else (r == 0))

    def first_axis_is_root(s, r, c):
        return s == 0 and r == 0

    def second_axis_is_root(s, r, c):
        return r == 0 if axis_of(1, c) == "z" else s == 0

    here = jnp.where((s == 0) & (r == 0), slab, jnp.zeros_like(slab))
    one = here
    for k in (1, 3, 2):
        one = one + permute(here, pairs(0, k, first_axis_is_root))
    two = one
    for k in (1, 3, 2):
        two = two + permute(one, pairs(1, k, second_axis_is_root))
    to_shard = []
    for g in range(16):
        for cc in range(8):
            b = 8 * g + cc
            to_shard.append((g * 8 + cc, (b % 16) * 8 + b // 16))
    panel_share = permute(share, to_shard)
    panel_share, two = lax.optimization_barrier((panel_share, two))
    ring_y = [two] + [permute(two, move_pairs("y", k)) for k in (1, 3, 2)]
    ring_y = jnp.stack([ring_y[0], ring_y[1], ring_y[2], ring_y[3]])
    corner = jnp.concatenate([ring_y, permute(ring_y, move_pairs("k", 1))], axis=0)

    arrived, corner = lax.optimization_barrier((arrived, corner))
    q_own = arrived[:, 32:]
    q_mate = permute(q_own, move_pairs("k", 1))
    row_share = jnp.concatenate([arrived[:, :32].reshape(16 * 32, K), share], axis=0)
    up_y = permute(row_share, move_pairs("y", 1))
    down_y = permute(row_share, move_pairs("y", -1))

    own_rows = lax.dynamic_slice_in_dim(panel, c * (E * B), E * B, 0).reshape(E, B, K)
    own_w = lax.dynamic_slice_in_dim(weights, c * E, E, 0)
    col_share = jnp.concatenate([(own_rows * own_w[:, None, :]).reshape(E * B, K), panel_share], axis=0)
    up, down = ring_near(col_share, 0)
    up, down, corner = lax.optimization_barrier((up, down, corner))
    line = stack_rows([col_share, up, down, *ring_far(up, down, 0)])
    line, corner = lax.optimization_barrier((line, corner))
    up, down = ring_near(line, 1)

    vmem = pl.BlockSpec(memory_space=pltpu.VMEM)
    smem = pl.BlockSpec(memory_space=pltpu.SMEM)
    half_done, upper, x_cat = pl.pallas_call(
        corner_kernel,
        in_specs=[smem, smem, vmem, vmem, vmem],
        out_specs=[vmem, vmem, vmem],
        out_shape=[
            jax.ShapeDtypeStruct((PW, PW), F32),
            jax.ShapeDtypeStruct((PW, PW), F32),
            jax.ShapeDtypeStruct((4, PW, 3 * K), BF16),
        ],
        scratch_shapes=[pltpu.VMEM((4, PW, 2 * K), BF16)],
        compiler_params=pltpu.CompilerParams(vmem_limit_bytes=40 * MIB),
        cost_estimate=pl.CostEstimate(flops=18_000_000_000, bytes_accessed=12 * MIB, transcendentals=0),
    )(idx, cmap, corner, q_own, q_mate)
    half_done, upper = middle_stage(1, half_done, upper)
    up_t, down_t, up_y, down_y, half_done = lax.optimization_barrier((up, down, up_y, down_y, half_done))
    far_a, far_b = ring_far(up_t, down_t, 1)
    far_y = (permute(up_y[:320], move_pairs("y", 1)), permute(down_y[320:], move_pairs("y", -1)))
    half_done, upper = middle_stage(2, half_done, upper)
    *far_y, far_a, far_b, half_done = lax.optimization_barrier((*far_y, far_a, far_b, half_done))
    row_data = stack_rows([row_share, up_y, down_y, *far_y])
    row_data, half_done = lax.optimization_barrier((row_data, half_done))
    row_mate = permute(row_data, move_pairs("k", 1)).reshape(4, 640, K)
    row_data = row_data.reshape(4, 640, K)
    lower, lower_inv = pl.pallas_call(
        finish_kernel,
        in_specs=[vmem, vmem],
        out_specs=[vmem, vmem],
        out_shape=[
            jax.ShapeDtypeStruct((PW, PW), F32),
            jax.ShapeDtypeStruct((PW, 3 * PW), BF16),
        ],
        scratch_shapes=[pltpu.VMEM((PW, PW), F32), pltpu.VMEM((PW, PW), F32)],
        compiler_params=pltpu.CompilerParams(vmem_limit_bytes=40 * MIB),
        cost_estimate=pl.CostEstimate(flops=12_000_000_000, bytes_accessed=5 * MIB, transcendentals=0),
    )(half_done, upper)

    def child_rows(i, idx, cmap):
        return (0, (idx[0] + offset(i)) % 4, 0)

    hbm = pl.BlockSpec(memory_space=pltpu.HBM)
    once = pl.Buffered(1)
    schur, own = pl.pallas_call(
        tile_kernel,
        grid_spec=pltpu.PrefetchScalarGridSpec(
            num_scalar_prefetch=2,
            grid=(4,),
            in_specs=[
                pl.BlockSpec((4, B, K), child_rows),
                pl.BlockSpec((4, B, K), child_rows),
                pl.BlockSpec((4, B, K), lambda i, idx, cmap: (0, 4, 0), pipeline_mode=once),
                pl.BlockSpec((4, B, K), lambda i, idx, cmap: (0, 4, 0), pipeline_mode=once),
                pl.BlockSpec((1, PW, 3 * K), lambda i, idx, cmap: (i, 0, 0)),
                pl.BlockSpec((PW, PW), lambda i, idx, cmap: (0, 0), pipeline_mode=once),
                pl.BlockSpec((PW, 3 * PW), lambda i, idx, cmap: (0, 0), pipeline_mode=once),
            ]
            + [hbm] * 6,
            out_specs=[hbm, hbm],
            scratch_shapes=[
                pltpu.VMEM((tile_rows + B, tile_cols), F32),
                pltpu.VMEM((tile_rows + B, PW), F32),
                pltpu.VMEM((tile_cols, PW), F32),
                pltpu.VMEM((tile_rows, 3 * K), BF16),
                pltpu.VMEM((tile_rows, 3 * K), BF16),
                pltpu.VMEM((256, 3 * K), BF16),
                pltpu.VMEM((2, 4, 3 * B, K), F32),
                pltpu.SemaphoreType.DMA((3,)),
                pltpu.SemaphoreType.DMA((2, 4)),
            ],
        ),
        out_shape=[
            jax.ShapeDtypeStruct((tile_rows, tile_cols), F32),
            jax.ShapeDtypeStruct((tile_rows, PW), F32),
        ],
        compiler_params=pltpu.CompilerParams(
            vmem_limit_bytes=56 * MIB, dimension_semantics=("arbitrary",)
        ),
        cost_estimate=pl.CostEstimate(flops=45_000_000_000, bytes_accessed=50 * MIB, transcendentals=0),
    )(idx, cmap, row_data, row_mate, row_data, row_mate, x_cat, lower, lower_inv, line, up_t, down_t, far_a, far_b, parent_front)
    return schur, own


def solution(mesh):
    placed = (P(("sub", "row"), "col"), P("sub", "row", None), P("sub", "row", None), P())
    return jax.shard_map(
        per_device,
        mesh=mesh,
        in_specs=placed,
        out_specs=(P(("sub", "row"), "col"), P(("sub", "row"), None)),
        check_vma=False,
    )
```
